512 devices in a mesh: lists: 64 (over z, y), users: 8 (over x, core).
Axes of the slice: x: 4, y: 4, z: 16, core: 2. Of those that a mesh axis runs over, the one named last changes fastest.
Arguments:
- user_vectors: bfloat16 [256, 512], P('lists'), may hold values from -6 to 6
- probe_lists: int32 [256, 32], P('lists'), may hold values from 0 to 63, as said below
- list_items: bfloat16 [64, 4096, 512], P('lists', 'users'), may hold values from -6 to 6
- candidate_ids: int32 [64, 512], P('lists'), may hold values from 0 to 262143, as said below
- history: bfloat16 [64, 1024, 512], P('lists', 'users'), may hold values from -6 to 6
- history_lengths: int32 [64], P('lists'), may hold values from 1 to 1024, as said below
- query_weight: bfloat16 [512, 512], replicated, may hold values from -4 to 4
- key_value_weight: bfloat16 [512, 1024], replicated, may hold values from -4 to 4
- out_weight: bfloat16 [512, 512], replicated, may hold values from -3 to 3
Outputs:
- list_scores: bfloat16 [256, 32, 4096], P('lists', None, 'users')
- ranked: bfloat16 [64, 512, 512], P('lists', 'users')
The draws below stay inside these ranges and needn't reach their ends.
Inputs may be any that keep to these rules, and one draw needn't show every extreme that they name: `probe_lists`: among the probes of the 4 users of one index of lists, no list occurs more than 6 times, and some list exactly 6 times. `candidate_ids`: item i lies in list i // 4096. Among the candidates of the 1 users of one index of lists, at most 3 lie in the same group of 1 lists (list) and the same group of 512 slots (slot // 512), and some such pair of groups holds exactly 3. `history_lengths`: the first ranked user has 1024 valid events.
All inputs are finite; a program needn't handle non-finite values.
Results may differ from the reference program's by a relative error of at most 0.018.
Values may be sent and summed in bfloat16 or wider, within the bound.
A program may use at most 128 MiB of HBM per device.

```python
import jax
import jax.numpy as jnp
from jax import lax

D = 512
HEADS = 8
LIST_DEV = 1
ITEMS_LIST = 4096
USER_DEV = 4
PROBES = 32
RANK_DEV = 1
CANDS = 512
LISTS = 64
ITEMS_LOC = 512
USERS = 256
RANK_USERS = 64
HIST = 1024
CAP_L = 6
CAP2 = 3


def capped_bins(key, blocks, count, bins, most):

    def one_block(block_key):
        hot_key, rest_key, order_key = jax.random.split(block_key, 3)
        hot = jax.random.randint(hot_key, (), 0, bins)
        stock = jnp.arange(bins * most, dtype=jnp.int32) // most
        others = jax.random.permutation(rest_key, stock[most:])
        chosen = jnp.concatenate([stock[:most], others[:count - most]])
        chosen = jax.random.permutation(order_key, chosen)
        return (chosen + hot) % bins
    return jax.vmap(one_block)(jax.random.split(key, blocks))


def shared_row(key):
    return jnp.clip(jax.random.normal(key, (D,), jnp.float32), -4.0, 4.0)


def draw_probe_lists(key, part):
    key = jax.random.fold_in(key, 11)
    chosen = capped_bins(key, USERS // USER_DEV, USER_DEV * PROBES, LISTS, CAP_L)
    return chosen.reshape(USERS, PROBES).astype(jnp.int32)


def draw_candidate_ids(key, part):
    key = jax.random.fold_in(key, 23)
    owner_key, list_key, slot_key = jax.random.split(key, 3)
    columns = ITEMS_LIST // ITEMS_LOC
    owners = capped_bins(owner_key, RANK_USERS // RANK_DEV, RANK_DEV * CANDS, LISTS // LIST_DEV * columns, CAP2)
    owners = owners.reshape(RANK_USERS, CANDS)
    row_owner = owners // columns
    col_owner = owners % columns
    sub_list = jax.random.randint(list_key, (RANK_USERS, CANDS), 0, LIST_DEV)
    sub_slot = jax.random.randint(slot_key, (RANK_USERS, CANDS), 0, ITEMS_LOC)
    list_id = row_owner * LIST_DEV + sub_list
    slot_id = col_owner * ITEMS_LOC + sub_slot
    return (list_id * ITEMS_LIST + slot_id).astype(jnp.int32)


def draw_history_lengths(key, part):
    key = jax.random.fold_in(key, 37)
    lengths = jax.random.randint(key, (RANK_USERS,), 1, HIST + 1)
    return lengths.at[0].set(HIST).astype(jnp.int32)


def draw_list_items(key, part):
    key = jax.random.fold_in(key, 53)
    shape = (LISTS, ITEMS_LIST, D)
    values = jnp.clip(jax.random.normal(key, shape, jnp.float32), -6.0, 6.0)
    return values.astype(jnp.bfloat16)


def draw_history(key, part):
    key = jax.random.fold_in(key, 59)
    shape = (RANK_USERS, HIST, D)
    values = jnp.clip(jax.random.normal(key, shape, jnp.float32), -6.0, 6.0)
    return values.astype(jnp.bfloat16)


def draw_query_weight(key, part):
    row = shared_row(key)
    key = jax.random.fold_in(key, 41)
    first = (jnp.arange(D, dtype=jnp.int32) == 0)[:, None]
    rest = jax.random.normal(key, (D, D), jnp.float32) * D ** (-0.5)
    lead = row * D ** (-0.5)
    return jnp.where(first, lead[None, :], rest).astype(jnp.bfloat16)


def draw_key_value_weight(key, part):
    key = jax.random.fold_in(key, 43)
    rest_key = jax.random.fold_in(key, 0)
    values = jax.random.normal(rest_key, (D, 2 * D), jnp.float32) * D ** (-0.5)
    return values.astype(jnp.bfloat16)


def block_levels(own_key, shape, pieces, low, top_value):
    def one(axis_at, shards_of):
        heights = jax.random.uniform(jax.random.fold_in(jax.random.fold_in(own_key, 6), axis_at), (shards_of,), jnp.float32, low / len(pieces), top_value / len(pieces))
        return jnp.repeat(jnp.exp(heights), shape[axis_at] // shards_of).reshape((-1,) + (1,) * (len(shape) - axis_at - 1))

    level = one(*pieces[0])
    for cut in pieces[1:]:
        level = level * one(*cut)
    return level


def normal_values(stream_key, extent, deviation, bound, pieces=(), kind=jnp.bfloat16):
    result = deviation * jax.random.normal(stream_key, extent, jnp.float32)
    if pieces:
        result = result * block_levels(stream_key, extent, pieces, -0.22, 0.18)
    return jnp.clip(result, -bound, bound).astype(kind)


def setup_inputs(seed: int = 0) -> dict:
    seeds = jax.random.split(jax.random.key(seed), 10)
    user_vectors = normal_values(seeds[0], (USERS, D), 1.0, 6.0, ((0, 64),))
    probe_lists = draw_probe_lists(jax.random.fold_in(seeds[9], 71), 0)
    list_items = draw_list_items(jax.random.fold_in(seeds[9], 71), 0)
    candidate_ids = draw_candidate_ids(jax.random.fold_in(seeds[9], 71), 0)
    history = draw_history(jax.random.fold_in(seeds[9], 71), 0)
    history_lengths = draw_history_lengths(jax.random.fold_in(seeds[9], 71), 0)
    query_weight = draw_query_weight(jax.random.fold_in(seeds[9], 71), 0)
    key_value_weight = draw_key_value_weight(jax.random.fold_in(seeds[9], 71), 0)
    out_weight = normal_values(seeds[8], (D, D), 0.5, 3.0)
    return {"user_vectors": user_vectors, "probe_lists": probe_lists, "list_items": list_items, "candidate_ids": candidate_ids, "history": history, "history_lengths": history_lengths, "query_weight": query_weight, "key_value_weight": key_value_weight, "out_weight": out_weight}


def reference(user_vectors, probe_lists, list_items, candidate_ids, history, history_lengths, query_weight, key_value_weight, out_weight):
    width = list_items.shape[2]
    scale = width ** -0.5

    def score_user(packed):
        vector, probes = packed
        blocks = list_items[probes].reshape(-1, width)
        scores = jnp.dot(blocks, vector[:, None], preferred_element_type=jnp.float32)[:, 0]
        return (scores * scale).reshape(probes.shape[0], -1).astype(jnp.bfloat16)

    list_scores = lax.map(score_user, (user_vectors, probe_lists))

    flat_items = list_items.reshape(-1, width)
    head_dim = width // HEADS

    def rank_user(packed):
        ids, events, length = packed
        rows = flat_items[ids]
        queries = (jnp.dot(rows, query_weight, preferred_element_type=jnp.float32) * head_dim ** -0.5).astype(jnp.bfloat16)
        queries = queries.reshape(-1, HEADS, head_dim).astype(jnp.float32)
        pairs = jnp.dot(events, key_value_weight, preferred_element_type=jnp.float32).astype(jnp.bfloat16)
        pairs = pairs.reshape(-1, 2, HEADS, head_dim).astype(jnp.float32)
        scores = jnp.einsum("chd,ehd->che", queries, pairs[:, 0], precision=lax.Precision.HIGHEST)
        valid = (jnp.arange(events.shape[0], dtype=jnp.int32) < length)[None, None, :]
        scores = jnp.where(valid, scores, jnp.float32(-1e30))
        top = jnp.max(scores, axis=-1)
        exponentials = jnp.where(valid, jnp.exp(scores - top[..., None]), jnp.float32(0.0))
        total = jnp.sum(exponentials, axis=-1)
        probs = lax.optimization_barrier(exponentials.astype(jnp.bfloat16)).astype(jnp.float32)
        mixed = jnp.einsum("che,ehd->chd", probs, pairs[:, 1], precision=lax.Precision.HIGHEST)
        attended = (mixed / total[..., None]).reshape(-1, width).astype(jnp.bfloat16)
        return jnp.dot(attended, out_weight, preferred_element_type=jnp.float32).astype(jnp.bfloat16)

    ranked = lax.map(rank_user, (candidate_ids, history, history_lengths))
    return list_scores, ranked
```

```python
import functools

import jax
import jax.numpy as jnp
from jax import lax
from jax.experimental import pallas as pl
from jax.experimental.pallas import tpu as pltpu
from jax.sharding import PartitionSpec as P

MESH = pl.DeviceIdType.MESH
F32 = jnp.float32
BF16 = jnp.bfloat16

L = 64
U = 8
X = 4
USERS = 4
PROBES = 32
ITEMS = 512
D = 512
SLOTS = 3
CANDS = 512
OWN = CANDS // U
EVENTS = 128
HIST = U * EVENTS
HEADS = 8
G = D // 128
ROWS = 16


def dot(a, b):
    return jnp.dot(a, b, preferred_element_type=F32)


def dot_first(a, b):
    return lax.dot_general(a, b, (((0,), (0,)), ((), ())), preferred_element_type=F32)


def dot_last(a, b):
    return lax.dot_general(a, b, (((1,), (1,)), ((), ())), preferred_element_type=F32)


def iota(shape, dim):
    return lax.broadcasted_iota(jnp.int32, shape, dim)


def kernel(
    ids,
    length,
    users,
    probes,
    items_hbm,
    history_hbm,
    wq_hbm,
    wkv_hbm,
    wo_hbm,
    list_scores,
    ranked,
    items,
    wq,
    wkv,
    wo,
    history,
    pairs,
    select,
    request,
    ask,
    asked,
    user_part,
    user_all,
    stage,
    rows_out,
    rows_in,
    scores_out,
    scores_in,
    placed,
    swap,
    spread,
    gathered,
    local_sem,
    send_sem,
    recv_sem,
):
    me = lax.axis_index("lists")
    col = lax.axis_index("users")
    chip, core = lax.div(col, 2), lax.rem(col, 2)

    def local(source, target, at):
        return pltpu.make_async_copy(source, target, local_sem.at[at])

    copies = [
        local(items_hbm, items, 0),
        local(history_hbm, history.at[col], 1),
        local(wkv_hbm, wkv, 2),
        local(wq_hbm, wq, 3),
        local(wo_hbm, wo, 4),
    ]
    for copy in copies:
        copy.start()

    barrier = pltpu.get_barrier_semaphore()

    @pl.loop(0, L)
    def _(p):
        @pl.when(p != me)
        def _():
            pl.semaphore_signal(barrier, inc=1, device_id=(p, col), device_id_type=MESH)

    @pl.loop(1, U)
    def _(d):
        pl.semaphore_signal(
            barrier, inc=1, device_id=(me, lax.rem(col + d, U)), device_id_type=MESH
        )

    wanted = ids[...]
    mine = lax.shift_right_logical(wanted, 9) == iota((L, CANDS), 0) * U + col
    mine = jnp.where(mine, 1.0, 0.0).astype(F32)
    place = jnp.bitwise_and(wanted, ITEMS - 1).astype(F32)
    earlier = jnp.where(iota((CANDS, CANDS), 0) < iota((CANDS, CANDS), 1), 1.0, 0.0)
    before = dot(mine.astype(BF16), earlier.astype(BF16))
    lane = iota((L, 128), 1)
    line = jnp.zeros((L, 128), F32)
    for k in range(SLOTS):
        chosen = jnp.where(before == k, mine, 0.0)
        select[k * L : (k + 1) * L, :] = chosen.astype(BF16)
        line = jnp.where(lane == k, jnp.sum(chosen * place, axis=1, keepdims=True), line)
    request[...] = line
    vectors = users[...].astype(F32)
    half = jnp.where(core == 0, vectors[:, :256], vectors[:, 256:])
    part = jnp.sum(jnp.where(iota((USERS, 256), 0) == chip, half, 0.0), axis=0, keepdims=True)

    @pl.loop(0, L)
    def _(p):
        ask[p, :, 0:128] = request[pl.ds(p, 1), :]
        ask[p, :, 128:384] = part

    stage[...] = jnp.zeros_like(stage)
    pl.semaphore_wait(barrier, L - 1 + U - 1)

    def to_rows(source, target, at):
        @pl.loop(1, L)
        def _(d):
            p = lax.rem(me + d, L)
            pltpu.make_async_remote_copy(
                source.at[p],
                target.at[me],
                send_sem.at[at],
                recv_sem.at[at],
                device_id=(p, col),
                device_id_type=MESH,
            ).start()

    def to_columns(source, target, at):
        @pl.loop(1, U)
        def _(d):
            pltpu.make_async_remote_copy(
                source,
                target.at[col],
                send_sem.at[at],
                recv_sem.at[at],
                device_id=(me, lax.rem(col + d, U)),
                device_id_type=MESH,
            ).start()

    def wait_all(target, count, sem):
        some = target.at[pl.ds(0, count)]
        pltpu.make_async_copy(some, some, sem).wait()

    to_rows(ask, asked, 0)
    copies[1].wait()
    to_columns(history.at[col], history, 1)
    asked[me] = ask[me]
    wait_all(asked, L - 1, recv_sem.at[0])

    @pl.loop(0, L)
    def _(p):
        request[pl.ds(p, 1), :] = asked[p, :, 0:128]
        user_part[pl.ds(p, 1), :] = asked[p, :, 128:384]

    user_all[col] = user_part[...].astype(BF16)
    to_columns(user_all.at[col], user_all, 2)

    copies[0].wait()
    asks = request[...]
    for k in range(SLOTS):
        hot = jnp.where(asks[:, k : k + 1] == iota((L, ITEMS), 1).astype(F32), 1.0, 0.0)
        found = dot(hot.astype(BF16), items[...])
        for g in range(G):
            stage[pl.ds(k * G + g, L, stride=ROWS), :] = found[:, g * 128 : (g + 1) * 128]
    rows_out[...] = stage[...].reshape(L, ROWS, 128).astype(BF16)
    rows_in[me] = rows_out[me]
    to_rows(rows_out, rows_in, 3)

    wait_all(user_all, U - 1, recv_sem.at[2])
    for u in range(USERS):
        found = dot_last(user_all[2 * u], items[:, 0:256]) + dot_last(
            user_all[2 * u + 1], items[:, 256:512]
        )
        found = found * D ** (-0.5)
        for g in range(G):
            stage[pl.ds(u * G + g, L, stride=ROWS), :] = found[:, g * 128 : (g + 1) * 128]
    scores_out[...] = stage[...].reshape(L, ROWS, 128).astype(BF16)
    scores_in[me] = scores_out[me]
    to_rows(scores_out, scores_in, 4)

    for copy in copies[2:]:
        copy.wait()
    wait_all(history, U - 1, recv_sem.at[1])

    @pl.loop(0, U)
    def _(c):
        pairs[pl.ds(pl.multiple_of(c * EVENTS, EVENTS), EVENTS), :] = dot(
            history[c], wkv[...]
        ).astype(BF16)

    wait_all(rows_in, L - 1, recv_sem.at[3])
    stage[...] = rows_in[...].astype(F32).reshape(L * ROWS, 128)
    for k in range(SLOTS):
        for g in range(G):
            gathered[k * L : (k + 1) * L, g * 128 : (g + 1) * 128] = stage[
                pl.ds(k * G + g, L, stride=ROWS), :
            ].astype(BF16)
    spots = dot_first(select[...], gathered[...]).astype(BF16)
    for c in range(U):
        placed[c % 2, c // 2] = spots[c * OWN : (c + 1) * OWN, :]
    first = pltpu.make_async_remote_copy(
        placed.at[1 - core],
        swap,
        send_sem.at[5],
        recv_sem.at[5],
        device_id=(me, 2 * chip + 1 - core),
        device_id_type=MESH,
    )
    first.start()
    first.wait_recv()
    spread[0:X] = (placed[core].astype(F32) + swap[...].astype(F32)).astype(BF16)

    @pl.loop(1, X)
    def _(d):
        there = lax.rem(chip + d, X)
        pltpu.make_async_remote_copy(
            spread.at[there],
            spread.at[X + d],
            send_sem.at[6],
            recv_sem.at[6],
            device_id=(me, 2 * there + core),
            device_id_type=MESH,
        ).start()

    wait_all(spread, X - 1, recv_sem.at[6])
    cand = spread[chip].astype(F32)
    for d in range(1, X):
        cand = cand + spread[X + d].astype(F32)

    queries = (dot(cand.astype(BF16), wq[...]) * (D // HEADS) ** (-0.5)).astype(BF16)
    low = iota((OWN, 128), 1) < 64
    valid = iota((1, HIST), 1) < length[0]
    nothing = jnp.zeros((OWN, 128), BF16)
    attended = []
    for j in range(HEADS // 2):
        two = queries[:, j * 128 : (j + 1) * 128]
        two = jnp.concatenate([jnp.where(low, two, nothing), jnp.where(low, nothing, two)], axis=0)
        scores = dot_last(two, pairs[:, j * 128 : (j + 1) * 128])
        scores = jnp.where(valid, scores, F32(-1e30))
        top = jnp.max(scores, axis=1, keepdims=True)
        powers = jnp.where(valid, jnp.exp(scores - top), 0.0)
        total = jnp.sum(powers, axis=1, keepdims=True)
        mixed = dot(powers.astype(BF16), pairs[:, D + j * 128 : D + (j + 1) * 128]) / total
        attended.append(jnp.where(low, mixed[:OWN], mixed[OWN:]).astype(BF16))
    ranked[...] = dot(jnp.concatenate(attended, axis=1), wo[...]).astype(BF16)

    wait_all(scores_in, L - 1, recv_sem.at[4])
    stage[...] = scores_in[...].astype(F32).reshape(L * ROWS, 128)
    for u in range(USERS):
        hot = jnp.where(iota((L, PROBES), 0) == probes[u : u + 1, :], 1.0, 0.0).astype(BF16)
        for g in range(G):
            found = stage[pl.ds(u * G + g, L, stride=ROWS), :].astype(BF16)
            list_scores[u, :, g * 128 : (g + 1) * 128] = dot_first(hot, found).astype(BF16)

    wait_all(asked, L - 1, send_sem.at[0])
    wait_all(history, U - 1, send_sem.at[1])
    wait_all(user_all, U - 1, send_sem.at[2])
    wait_all(rows_in, L - 1, send_sem.at[3])
    wait_all(scores_in, L - 1, send_sem.at[4])
    first.wait_send()
    wait_all(spread, X - 1, send_sem.at[6])


def shards(
    user_vectors,
    probe_lists,
    list_items,
    candidate_ids,
    history,
    history_lengths,
    query_weight,
    key_value_weight,
    out_weight,
):
    vmem = pl.BlockSpec(memory_space=pltpu.VMEM)
    smem = pl.BlockSpec(memory_space=pltpu.SMEM)
    hbm = pl.BlockSpec(memory_space=pl.ANY)
    list_scores, ranked = pl.pallas_call(
        kernel,
        out_shape=(
            jax.ShapeDtypeStruct((USERS, PROBES, ITEMS), BF16),
            jax.ShapeDtypeStruct((OWN, D), BF16),
        ),
        in_specs=[vmem, smem, vmem, vmem, hbm, hbm, hbm, hbm, hbm],
        out_specs=(vmem, vmem),
        scratch_shapes=[
            pltpu.VMEM((ITEMS, D), BF16),
            pltpu.VMEM((D, D), BF16),
            pltpu.VMEM((D, 2 * D), BF16),
            pltpu.VMEM((D, D), BF16),
            pltpu.VMEM((U, EVENTS, D), BF16),
            pltpu.VMEM((HIST, 2 * D), BF16),
            pltpu.VMEM((SLOTS * L, CANDS), BF16),
            pltpu.VMEM((L, 128), F32),
            pltpu.VMEM((L, 1, 384), F32),
            pltpu.VMEM((L, 1, 384), F32),
            pltpu.VMEM((L, 256), F32),
            pltpu.VMEM((U, L, 256), BF16),
            pltpu.VMEM((L * ROWS, 128), F32),
            pltpu.VMEM((L, ROWS, 128), BF16),
            pltpu.VMEM((L, ROWS, 128), BF16),
            pltpu.VMEM((L, ROWS, 128), BF16),
            pltpu.VMEM((L, ROWS, 128), BF16),
            pltpu.VMEM((2, X, OWN, D), BF16),
            pltpu.VMEM((X, OWN, D), BF16),
            pltpu.VMEM((2 * X, OWN, D), BF16),
            pltpu.VMEM((SLOTS * L, D), BF16),
            pltpu.SemaphoreType.DMA((5,)),
            pltpu.SemaphoreType.DMA((7,)),
            pltpu.SemaphoreType.DMA((7,)),
        ],
        compiler_params=pltpu.CompilerParams(
            collective_id=0, has_side_effects=True, vmem_limit_bytes=56 * 2**20
        ),
        cost_estimate=pl.CostEstimate(
            flops=2 * 10**9, bytes_accessed=4 * 10**6, transcendentals=600000
        ),
    )(
        candidate_ids,
        history_lengths,
        user_vectors,
        probe_lists,
        list_items.reshape(ITEMS, D),
        history.reshape(EVENTS, D),
        query_weight,
        key_value_weight,
        out_weight,
    )
    return list_scores, ranked.reshape(1, OWN, D)


def solution(mesh):
    placed = (
        P("lists", None),
        P("lists", None),
        P("lists", "users", None),
        P("lists", None),
        P("lists", "users", None),
        P("lists"),
        P(),
        P(),
        P(),
    )
    return jax.shard_map(
        shards,
        mesh=mesh,
        in_specs=placed,
        out_specs=(P("lists", None, "users"), P("lists", "users", None)),
        check_vma=False,
    )
```

```python
import jax
import jax.numpy as jnp
from jax import lax
from jax.experimental import pallas as pl
from jax.experimental.pallas import tpu as pltpu
from jax.sharding import PartitionSpec as P

MESH = pl.DeviceIdType.MESH
F32 = jnp.float32
BF16 = jnp.bfloat16

L = 64
U = 8
X = 4
USERS = 4
PROBES = 32
ITEMS = 512
D = 512
SLOTS = 3
CANDS = 512
OWN = CANDS // U
EVENTS = 128
HIST = U * EVENTS
HEADS = 8
G = D // 128
ROWS = 16


def dot(a, b):
    return jnp.dot(a, b, preferred_element_type=F32)


def dot_first(a, b):
    return lax.dot_general(a, b, (((0,), (0,)), ((), ())), preferred_element_type=F32)


def dot_last(a, b):
    return lax.dot_general(a, b, (((1,), (1,)), ((), ())), preferred_element_type=F32)


def iota(shape, dim):
    return lax.broadcasted_iota(jnp.int32, shape, dim)


def kernel(
    ids_hbm,
    length_hbm,
    users_hbm,
    items_hbm,
    history_hbm,
    wq_hbm,
    wkv_hbm,
    wo_hbm,
    scores_in,
    ranked,
    ids,
    length,
    users,
    items,
    wq,
    wkv,
    wo,
    history,
    pairs,
    select,
    request,
    ask,
    asked,
    part,
    parts,
    user_part,
    user_all,
    stage,
    rows_out,
    rows_in,
    scores_out,
    placed,
    swap,
    spread,
    gathered,
    local_sem,
    send_sem,
    recv_sem,
):
    me = lax.axis_index("lists")
    col = lax.axis_index("users")
    chip, core = lax.div(col, 2), lax.rem(col, 2)

    def local(source, target, at):
        return pltpu.make_async_copy(source, target, local_sem.at[at])

    get_ids = local(ids_hbm, ids, 0)
    get_users = local(users_hbm, users, 1)
    get_history = local(history_hbm, history.at[col], 2)
    get_items = local(items_hbm, items, 3)
    get_rest = [
        local(wkv_hbm, wkv, 4),
        local(wq_hbm, wq, 5),
        local(wo_hbm, wo, 6),
        local(length_hbm, length, 7),
    ]
    get_ids.start()
    get_users.start()
    get_history.start()

    barrier = pltpu.get_barrier_semaphore()

    @pl.loop(0, L)
    def _(p):
        @pl.when(p != me)
        def _():
            pl.semaphore_signal(barrier, inc=1, device_id=(p, col), device_id_type=MESH)

    @pl.loop(1, U)
    def _(d):
        pl.semaphore_signal(
            barrier, inc=1, device_id=(me, lax.rem(col + d, U)), device_id_type=MESH
        )

    get_items.start()
    for copy in get_rest:
        copy.start()

    get_ids.wait()
    wanted = ids[...]
    mine = lax.shift_right_logical(wanted, 9) == iota((L, CANDS), 0) * U + col
    mine = jnp.where(mine, 1.0, 0.0).astype(F32)
    place = jnp.bitwise_and(wanted, ITEMS - 1).astype(F32)
    earlier = jnp.where(iota((CANDS, CANDS), 0) < iota((CANDS, CANDS), 1), 1.0, 0.0)
    before = dot(mine.astype(BF16), earlier.astype(BF16))
    lane = iota((L, 128), 1)
    line = jnp.zeros((L, 128), F32)
    slots = []
    for k in range(SLOTS):
        slots.append(jnp.where(before == k, mine, 0.0))
        line = jnp.where(lane == k, jnp.sum(slots[k] * place, axis=1, keepdims=True), line)
    request[...] = line

    @pl.loop(0, L)
    def _(p):
        ask[p] = request[pl.ds(p, 1), :]

    get_users.wait()
    vectors = users[...].astype(F32)
    half = jnp.where(core == 0, vectors[:, :256], vectors[:, 256:])
    part[0] = jnp.sum(jnp.where(iota((USERS, 256), 0) == chip, half, 0.0), axis=0, keepdims=True)
    get_history.wait()
    pl.semaphore_wait(barrier, L - 1 + U - 1)

    def to_rows(source, target, at, order):
        def send(p):
            pltpu.make_async_remote_copy(
                source(p),
                target.at[me],
                send_sem.at[at],
                recv_sem.at[at],
                device_id=(p, col),
                device_id_type=MESH,
            ).start()

        if order is None:

            @pl.loop(1, L)
            def _(d):
                send(lax.rem(me + d, L))

        else:
            for first, count, rotate in order:
                @pl.loop(0, 4 * count)
                def _(i):
                    if rotate:
                        i = lax.rem(i + me + 4 * rotate, 4 * count)
                    p = 4 * first + i
                    @pl.when(p != me)
                    def _():
                        send(p)

    def to_chips(source, target, at):
        @pl.loop(1, X)
        def _(d):
            there = lax.rem(chip + d, X)
            pltpu.make_async_remote_copy(
                source(there),
                target(d),
                send_sem.at[at],
                recv_sem.at[at],
                device_id=(me, 2 * there + core),
                device_id_type=MESH,
            ).start()

    def to_core(source, target, at):
        return pltpu.make_async_remote_copy(
            source,
            target,
            send_sem.at[at],
            recv_sem.at[at],
            device_id=(me, 2 * chip + 1 - core),
            device_id_type=MESH,
        )

    def wait_all(target, count, sem):
        some = target.at[pl.ds(0, count)]
        pltpu.make_async_copy(some, some, sem).wait()

    to_rows(lambda p: ask.at[p], asked, 0, None)
    to_chips(lambda there: history.at[col], lambda d: history.at[col], 1)
    to_rows(lambda p: part.at[0], parts, 2, None)
    asked[me] = ask[me]
    parts[me] = part[0]

    turned = jnp.concatenate(slots + [jnp.zeros((L, CANDS), F32)], axis=0).T.astype(BF16)
    for c in range(U):
        at = (c % 2) * X + c // 2
        select[at * OWN : (at + 1) * OWN, :] = turned[c * OWN : (c + 1) * OWN, :]
    gathered[SLOTS * L :, :] = jnp.zeros((L, D), BF16)
    stage[...] = jnp.zeros_like(stage)

    get_items.wait()
    wait_all(asked, L - 1, recv_sem.at[0])

    @pl.loop(0, L)
    def _(p):
        request[pl.ds(p, 1), :] = asked[p]

    asks = request[...]
    for k in range(SLOTS):
        hot = jnp.where(asks[:, k : k + 1] == iota((L, ITEMS), 1).astype(F32), 1.0, 0.0)
        found = dot(hot.astype(BF16), items[...])
        for g in range(G):
            stage[pl.ds(k * G + g, L, stride=ROWS), :] = found[:, g * 128 : (g + 1) * 128]
    rows_out[...] = stage[...].reshape(L, ROWS, 128).astype(BF16)
    to_rows(lambda p: rows_out.at[p], rows_in, 3, [(0, 4, 1), (4, 4, 1), (12, 4, 1), (8, 4, 1)])
    rows_in[me] = rows_out[me]

    wait_all(parts, L - 1, recv_sem.at[2])

    @pl.loop(0, L)
    def _(p):
        user_part[pl.ds(p, 1), :] = parts[p]

    user_all[col] = user_part[...].astype(BF16)

    @pl.loop(1, U)
    def _(d):
        pltpu.make_async_remote_copy(
            user_all.at[col],
            user_all.at[col],
            send_sem.at[4],
            recv_sem.at[4],
            device_id=(me, lax.rem(col + d, U)),
            device_id_type=MESH,
        ).start()

    wait_all(history, X - 1, recv_sem.at[1])

    @pl.loop(0, X)
    def _(x):
        to_core(history.at[2 * x + core], history.at[2 * x + core], 5).start()

    for copy in get_rest:
        copy.wait()
    wait_all(history, X, recv_sem.at[5])

    @pl.loop(0, U)
    def _(c):
        pairs[pl.ds(pl.multiple_of(c * EVENTS, EVENTS), EVENTS), :] = dot(
            history[c], wkv[...]
        ).astype(BF16)

    wait_all(user_all, U - 1, recv_sem.at[4])
    for u in range(USERS):
        found = dot_last(user_all[2 * u], items[:, 0:256]) + dot_last(
            user_all[2 * u + 1], items[:, 256:512]
        )
        found = found * D ** (-0.5)
        for g in range(G):
            stage[pl.ds(u * G + g, L, stride=ROWS), :] = found[:, g * 128 : (g + 1) * 128]
    scores_out[...] = stage[...].reshape(L, ROWS, 128).astype(BF16)
    keep = local(scores_out.at[me], scores_in.at[me], 8)
    keep.start()
    to_rows(lambda p: scores_out.at[p], scores_in, 6, None)

    wait_all(rows_in, L - 1, recv_sem.at[3])
    stage[...] = rows_in[...].astype(F32).reshape(L * ROWS, 128)
    for k in range(SLOTS):
        for g in range(G):
            gathered[k * L : (k + 1) * L, g * 128 : (g + 1) * 128] = stage[
                pl.ds(k * G + g, L, stride=ROWS), :
            ].astype(BF16)

    def spots(c):
        block = select[pl.ds(pl.multiple_of(c * X * OWN, X * OWN), X * OWN), :]
        return dot(block, gathered[...])

    placed[...] = spots(1 - core).astype(BF16).reshape(X, OWN, D)
    pair = to_core(placed, swap, 7)
    pair.start()
    kept = spots(core).reshape(X, OWN, D)
    pair.wait_recv()
    spread[0:X] = (kept + swap[...].astype(F32)).astype(BF16)
    to_chips(lambda there: spread.at[there], lambda d: spread.at[X + d], 8)
    wait_all(spread, X - 1, recv_sem.at[8])
    cand = spread[chip].astype(F32)
    for d in range(1, X):
        cand = cand + spread[X + d].astype(F32)

    queries = (dot(cand.astype(BF16), wq[...]) * (D // HEADS) ** (-0.5)).astype(BF16)
    low = iota((OWN, 128), 1) < 64
    valid = iota((1, HIST), 1) < length[0]
    nothing = jnp.zeros((OWN, 128), BF16)
    attended = []
    for j in range(HEADS // 2):
        two = queries[:, j * 128 : (j + 1) * 128]
        two = jnp.concatenate([jnp.where(low, two, nothing), jnp.where(low, nothing, two)], axis=0)
        scores = dot_last(two, pairs[:, j * 128 : (j + 1) * 128])
        scores = jnp.where(valid, scores, F32(-1e30))
        top = jnp.max(scores, axis=1, keepdims=True)
        powers = jnp.where(valid, jnp.exp(scores - top), 0.0)
        total = jnp.sum(powers, axis=1, keepdims=True)
        mixed = dot(powers.astype(BF16), pairs[:, D + j * 128 : D + (j + 1) * 128]) / total
        attended.append(jnp.where(low, mixed[:OWN], mixed[OWN:]).astype(BF16))
    ranked[...] = dot(jnp.concatenate(attended, axis=1), wo[...]).astype(BF16)

    wait_all(asked, L - 1, send_sem.at[0])
    wait_all(history, X - 1, send_sem.at[1])
    wait_all(parts, L - 1, send_sem.at[2])
    wait_all(rows_in, L - 1, send_sem.at[3])
    wait_all(user_all, U - 1, send_sem.at[4])
    wait_all(history, X, send_sem.at[5])
    pair.wait_send()
    wait_all(spread, X - 1, send_sem.at[8])
    keep.wait()
    wait_all(scores_in, L - 1, send_sem.at[6])
    wait_all(scores_in, L - 1, recv_sem.at[6])


def finish(
    probes_hbm, scores_hbm, ranked_hbm, list_scores, ranked, probes, scores, stage, sem
):
    copies = [
        pltpu.make_async_copy(scores_hbm, scores, sem.at[0]),
        pltpu.make_async_copy(probes_hbm, probes, sem.at[1]),
        pltpu.make_async_copy(ranked_hbm, ranked, sem.at[2]),
    ]
    for copy in copies:
        copy.start()
    copies[1].wait()
    copies[0].wait()
    stage[...] = scores[...].astype(F32).reshape(L * ROWS, 128)
    for u in range(USERS):
        hot = jnp.where(iota((L, PROBES), 0) == probes[u : u + 1, :], 1.0, 0.0).astype(BF16)
        found = [stage[pl.ds(u * G + g, L, stride=ROWS), :].astype(BF16) for g in range(G)]
        list_scores[u] = dot_first(hot, jnp.concatenate(found, axis=1)).astype(BF16)
    copies[2].wait()


def shards(
    user_vectors,
    probe_lists,
    list_items,
    candidate_ids,
    history,
    history_lengths,
    query_weight,
    key_value_weight,
    out_weight,
):
    vmem = pl.BlockSpec(memory_space=pltpu.VMEM)
    hbm = pl.BlockSpec(memory_space=pl.ANY)
    scores_in, ranked = pl.pallas_call(
        kernel,
        out_shape=(
            jax.ShapeDtypeStruct((L, ROWS, 128), BF16),
            jax.ShapeDtypeStruct((OWN, D), BF16),
        ),
        in_specs=[hbm] * 8,
        out_specs=(hbm, vmem),
        scratch_shapes=[
            pltpu.VMEM((1, CANDS), jnp.int32),
            pltpu.SMEM((1,), jnp.int32),
            pltpu.VMEM((USERS, D), BF16),
            pltpu.VMEM((ITEMS, D), BF16),
            pltpu.VMEM((D, D), BF16),
            pltpu.VMEM((D, 2 * D), BF16),
            pltpu.VMEM((D, D), BF16),
            pltpu.VMEM((U, EVENTS, D), BF16),
            pltpu.VMEM((HIST, 2 * D), BF16),
            pltpu.VMEM((CANDS, 4 * L), BF16),
            pltpu.VMEM((L, 128), F32),
            pltpu.VMEM((L, 1, 128), F32),
            pltpu.VMEM((L, 1, 128), F32),
            pltpu.VMEM((1, 1, 256), F32),
            pltpu.VMEM((L, 1, 256), F32),
            pltpu.VMEM((L, 256), F32),
            pltpu.VMEM((U, L, 256), BF16),
            pltpu.VMEM((L * ROWS, 128), F32),
            pltpu.VMEM((L, ROWS, 128), BF16),
            pltpu.VMEM((L, ROWS, 128), BF16),
            pltpu.VMEM((L, ROWS, 128), BF16),
            pltpu.VMEM((X, OWN, D), BF16),
            pltpu.VMEM((X, OWN, D), BF16),
            pltpu.VMEM((2 * X, OWN, D), BF16),
            pltpu.VMEM((4 * L, D), BF16),
            pltpu.SemaphoreType.DMA((9,)),
            pltpu.SemaphoreType.DMA((9,)),
            pltpu.SemaphoreType.DMA((9,)),
        ],
        compiler_params=pltpu.CompilerParams(
            collective_id=0, has_side_effects=True, vmem_limit_bytes=56 * 2**20
        ),
        cost_estimate=pl.CostEstimate(
            flops=2 * 10**9, bytes_accessed=4 * 10**6, transcendentals=600000
        ),
    )(
        candidate_ids,
        history_lengths,
        user_vectors,
        list_items.reshape(ITEMS, D),
        history.reshape(EVENTS, D),
        query_weight,
        key_value_weight,
        out_weight,
    )
    list_scores, ranked = pl.pallas_call(
        finish,
        out_shape=(
            jax.ShapeDtypeStruct((USERS, PROBES, ITEMS), BF16),
            jax.ShapeDtypeStruct((OWN, D), BF16),
        ),
        in_specs=[hbm] * 3,
        out_specs=(vmem, vmem),
        scratch_shapes=[
            pltpu.VMEM((USERS, PROBES), jnp.int32),
            pltpu.VMEM((L, ROWS, 128), BF16),
            pltpu.VMEM((L * ROWS, 128), F32),
            pltpu.SemaphoreType.DMA((3,)),
        ],
        compiler_params=pltpu.CompilerParams(vmem_limit_bytes=56 * 2**20),
        cost_estimate=pl.CostEstimate(flops=2 * 10**7, bytes_accessed=10**6, transcendentals=0),
    )(probe_lists, scores_in, ranked)
    return list_scores, ranked.reshape(1, OWN, D)


def solution(mesh):
    placed = (
        P("lists", None),
        P("lists", None),
        P("lists", "users", None),
        P("lists", None),
        P("lists", "users", None),
        P("lists"),
        P(),
        P(),
        P(),
    )
    return jax.shard_map(
        shards,
        mesh=mesh,
        in_specs=placed,
        out_specs=(P("lists", None, "users"), P("lists", "users", None)),
        check_vma=False,
    )
```

```python
import jax
import jax.numpy as jnp
from jax import lax
from jax.experimental import pallas as pl
from jax.experimental.pallas import tpu as pltpu
from jax.sharding import PartitionSpec as P

MESH = pl.DeviceIdType.MESH
F32 = jnp.float32
BF16 = jnp.bfloat16

L = 64
Z = 16
U = 8
X = 4
USERS = 4
PROBES = 32
ITEMS = 512
D = 512
SLOTS = 3
CANDS = 512
OWN = CANDS // U
EVENTS = 128
HIST = U * EVENTS
HEADS = 8
G = D // 128
ROWS = 16


def dot(a, b):
    return jnp.dot(a, b, preferred_element_type=F32)


def dot_first(a, b):
    return lax.dot_general(a, b, (((0,), (0,)), ((), ())), preferred_element_type=F32)


def dot_last(a, b):
    return lax.dot_general(a, b, (((1,), (1,)), ((), ())), preferred_element_type=F32)


def iota(shape, dim):
    return lax.broadcasted_iota(jnp.int32, shape, dim)


def kernel(
    ids_hbm,
    length_hbm,
    users_hbm,
    items_hbm,
    history_hbm,
    wq_hbm,
    wkv_hbm,
    wo_hbm,
    scores_in,
    ranked,
    ids,
    length,
    users,
    items,
    wq,
    wkv,
    wo,
    history,
    pairs,
    select,
    request,
    ask,
    asked,
    part,
    parts,
    user_part,
    user_plane,
    user_all,
    stage,
    rows_out,
    rows_in,
    scores_out,
    placed,
    swap,
    spread,
    gathered,
    local_sem,
    send_sem,
    recv_sem,
    heard,
):
    me = lax.axis_index("lists")
    col = lax.axis_index("users")
    chip, core = lax.div(col, 2), lax.rem(col, 2)
    plane, row = lax.div(me, 4), lax.rem(me, 4)

    def local(source, target, at):
        return pltpu.make_async_copy(source, target, local_sem.at[at])

    get_ids = local(ids_hbm, ids, 0)
    get_users = local(users_hbm, users, 1)
    get_history = local(history_hbm, history.at[col], 2)
    get_items = local(items_hbm, items, 3)
    get_rest = [
        local(wkv_hbm, wkv, 4),
        local(wq_hbm, wq, 5),
        local(wo_hbm, wo, 6),
        local(length_hbm, length, 7),
    ]
    get_ids.start()
    get_users.start()
    get_history.start()

    barrier = pltpu.get_barrier_semaphore()

    def over_z(d):
        return lax.rem(me + 4 * d, L)

    def over_y(d):
        return me - row + lax.rem(row + d, 4)

    for d in range(1, Z):
        pl.semaphore_signal(barrier, inc=1, device_id=(over_z(d), col), device_id_type=MESH)
    for d in range(1, 4):
        pl.semaphore_signal(barrier, inc=1, device_id=(over_y(d), col), device_id_type=MESH)

    @pl.loop(1, U)
    def _(d):
        pl.semaphore_signal(
            barrier, inc=1, device_id=(me, lax.rem(col + d, U)), device_id_type=MESH
        )

    get_items.start()
    for copy in get_rest:
        copy.start()

    get_ids.wait()
    wanted = ids[...]
    mine = lax.shift_right_logical(wanted, 9) == iota((L, CANDS), 0) * U + col
    mine = jnp.where(mine, 1.0, 0.0).astype(F32)
    place = jnp.bitwise_and(wanted, ITEMS - 1).astype(F32)
    earlier = jnp.where(iota((CANDS, CANDS), 0) < iota((CANDS, CANDS), 1), 1.0, 0.0)
    before = dot(mine.astype(BF16), earlier.astype(BF16))
    lane = iota((L, 128), 1)
    line = jnp.zeros((L, 128), F32)
    slots = []
    for k in range(SLOTS):
        slots.append(jnp.where(before == k, mine, 0.0))
        line = jnp.where(lane == k, jnp.sum(slots[k] * place, axis=1, keepdims=True), line)
    request[...] = line

    @pl.loop(0, L)
    def _(p):
        ask[p] = request[pl.ds(p, 1), :]

    get_users.wait()
    vectors = users[...].astype(F32)
    half = jnp.where(core == 0, vectors[:, :256], vectors[:, 256:])
    part[0] = jnp.sum(jnp.where(iota((USERS, 256), 0) == chip, half, 0.0), axis=0, keepdims=True)
    get_history.wait()
    pl.semaphore_wait(barrier, Z - 1 + 4 - 1 + U - 1)
    for d in range(1, 4):
        pl.semaphore_signal(heard, inc=1, device_id=(over_y(d), col), device_id_type=MESH)
    pl.semaphore_wait(heard, 4 - 1)

    def to_rows(source, target, at, order):
        def send(p):
            pltpu.make_async_remote_copy(
                source(p),
                target.at[me],
                send_sem.at[at],
                recv_sem.at[at],
                device_id=(p, col),
                device_id_type=MESH,
            ).start()

        if order is None:

            @pl.loop(1, L)
            def _(d):
                send(lax.rem(me + d, L))

        else:
            for first, count, rotate in order:
                @pl.loop(0, 4 * count)
                def _(i):
                    if rotate:
                        i = lax.rem(i + me + 4 * rotate, 4 * count)
                    p = 4 * first + i
                    @pl.when(p != me)
                    def _():
                        send(p)

    def to_chips(source, target, at):
        @pl.loop(1, X)
        def _(d):
            there = lax.rem(chip + d, X)
            pltpu.make_async_remote_copy(
                source(there),
                target(d),
                send_sem.at[at],
                recv_sem.at[at],
                device_id=(me, 2 * there + core),
                device_id_type=MESH,
            ).start()

    def to_core(source, target, at):
        return pltpu.make_async_remote_copy(
            source,
            target,
            send_sem.at[at],
            recv_sem.at[at],
            device_id=(me, 2 * chip + 1 - core),
            device_id_type=MESH,
        )

    def wait_all(target, count, sem):
        some = target.at[pl.ds(0, count)]
        pltpu.make_async_copy(some, some, sem).wait()

    to_rows(lambda p: ask.at[p], asked, 0, None)
    to_chips(lambda there: history.at[col], lambda d: history.at[col], 1)
    for d in range(1, Z):
        pltpu.make_async_remote_copy(
            part.at[0],
            parts.at[plane],
            send_sem.at[2],
            recv_sem.at[2],
            device_id=(over_z(d), col),
            device_id_type=MESH,
        ).start()
    asked[me] = ask[me]
    parts[plane] = part[0]

    turned = jnp.concatenate(slots + [jnp.zeros((L, CANDS), F32)], axis=0).T.astype(BF16)
    for c in range(U):
        at = (c % 2) * X + c // 2
        select[at * OWN : (at + 1) * OWN, :] = turned[c * OWN : (c + 1) * OWN, :]
    gathered[SLOTS * L :, :] = jnp.zeros((L, D), BF16)
    stage[...] = jnp.zeros_like(stage)

    get_items.wait()
    wait_all(asked, L - 1, recv_sem.at[0])

    @pl.loop(0, L)
    def _(p):
        request[pl.ds(p, 1), :] = asked[p]

    asks = request[...]
    for k in range(SLOTS):
        hot = jnp.where(asks[:, k : k + 1] == iota((L, ITEMS), 1).astype(F32), 1.0, 0.0)
        found = dot(hot.astype(BF16), items[...])
        for g in range(G):
            stage[pl.ds(k * G + g, L, stride=ROWS), :] = found[:, g * 128 : (g + 1) * 128]
    rows_out[...] = stage[...].reshape(L, ROWS, 128).astype(BF16)
    to_rows(lambda p: rows_out.at[p], rows_in, 3, [(0, 4, 1), (4, 12, 1)])
    rows_in[me] = rows_out[me]

    wait_all(parts, Z - 1, recv_sem.at[2])
    for z in range(Z):
        user_part[z : z + 1, :] = parts[z]
    user_plane[row] = user_part[...].astype(BF16)
    for d in range(1, 4):
        pltpu.make_async_remote_copy(
            user_plane.at[row],
            user_plane.at[row],
            send_sem.at[9],
            recv_sem.at[9],
            device_id=(over_y(d), col),
            device_id_type=MESH,
        ).start()

    wait_all(history, X - 1, recv_sem.at[1])

    @pl.loop(0, X)
    def _(x):
        to_core(history.at[2 * x + core], history.at[2 * x + core], 5).start()

    wait_all(user_plane, 4 - 1, recv_sem.at[9])
    user_all[col] = user_plane[...].reshape(L, 256)

    @pl.loop(1, U)
    def _(d):
        pltpu.make_async_remote_copy(
            user_all.at[col],
            user_all.at[col],
            send_sem.at[4],
            recv_sem.at[4],
            device_id=(me, lax.rem(col + d, U)),
            device_id_type=MESH,
        ).start()

    for copy in get_rest:
        copy.wait()
    wait_all(history, X, recv_sem.at[5])

    @pl.loop(0, U)
    def _(c):
        pairs[pl.ds(pl.multiple_of(c * EVENTS, EVENTS), EVENTS), :] = dot(
            history[c], wkv[...]
        ).astype(BF16)

    wait_all(user_all, U - 1, recv_sem.at[4])
    for u in range(USERS):
        found = dot_last(user_all[2 * u], items[:, 0:256]) + dot_last(
            user_all[2 * u + 1], items[:, 256:512]
        )
        found = found * D ** (-0.5)
        for y in range(4):
            for g in range(G):
                stage[pl.ds(y * ROWS + u * G + g, Z, stride=4 * ROWS), :] = found[
                    y * Z : (y + 1) * Z, g * 128 : (g + 1) * 128
                ]
    scores_out[...] = stage[...].reshape(L, ROWS, 128).astype(BF16)
    keep = local(scores_out.at[me], scores_in.at[me], 8)
    keep.start()
    to_rows(lambda p: scores_out.at[p], scores_in, 6, [(0, 16, 0)])

    wait_all(rows_in, L - 1, recv_sem.at[3])
    stage[...] = rows_in[...].astype(F32).reshape(L * ROWS, 128)
    for k in range(SLOTS):
        for g in range(G):
            gathered[k * L : (k + 1) * L, g * 128 : (g + 1) * 128] = stage[
                pl.ds(k * G + g, L, stride=ROWS), :
            ].astype(BF16)

    def spots(c):
        block = select[pl.ds(pl.multiple_of(c * X * OWN, X * OWN), X * OWN), :]
        return dot(block, gathered[...])

    placed[...] = spots(1 - core).astype(BF16).reshape(X, OWN, D)
    pair = to_core(placed, swap, 7)
    pair.start()
    kept = spots(core).reshape(X, OWN, D)
    pair.wait_recv()
    spread[0:X] = (kept + swap[...].astype(F32)).astype(BF16)
    to_chips(lambda there: spread.at[there], lambda d: spread.at[X + d], 8)
    wait_all(spread, X - 1, recv_sem.at[8])
    cand = spread[chip].astype(F32)
    for d in range(1, X):
        cand = cand + spread[X + d].astype(F32)

    queries = (dot(cand.astype(BF16), wq[...]) * (D // HEADS) ** (-0.5)).astype(BF16)
    low = iota((OWN, 128), 1) < 64
    valid = iota((1, HIST), 1) < length[0]
    nothing = jnp.zeros((OWN, 128), BF16)
    attended = []
    for j in range(HEADS // 2):
        two = queries[:, j * 128 : (j + 1) * 128]
        two = jnp.concatenate([jnp.where(low, two, nothing), jnp.where(low, nothing, two)], axis=0)
        scores = dot_last(two, pairs[:, j * 128 : (j + 1) * 128])
        scores = jnp.where(valid, scores, F32(-1e30))
        top = jnp.max(scores, axis=1, keepdims=True)
        powers = jnp.where(valid, jnp.exp(scores - top), 0.0)
        total = jnp.sum(powers, axis=1, keepdims=True)
        mixed = dot(powers.astype(BF16), pairs[:, D + j * 128 : D + (j + 1) * 128]) / total
        attended.append(jnp.where(low, mixed[:OWN], mixed[OWN:]).astype(BF16))
    ranked[...] = dot(jnp.concatenate(attended, axis=1), wo[...]).astype(BF16)

    wait_all(asked, L - 1, send_sem.at[0])
    wait_all(history, X - 1, send_sem.at[1])
    wait_all(parts, Z - 1, send_sem.at[2])
    wait_all(user_plane, 4 - 1, send_sem.at[9])
    wait_all(rows_in, L - 1, send_sem.at[3])
    wait_all(user_all, U - 1, send_sem.at[4])
    wait_all(history, X, send_sem.at[5])
    pair.wait_send()
    wait_all(spread, X - 1, send_sem.at[8])
    keep.wait()
    wait_all(scores_in, L - 1, send_sem.at[6])
    wait_all(scores_in, L - 1, recv_sem.at[6])


def finish(
    probes_hbm, scores_hbm, ranked_hbm, list_scores, ranked, probes, scores, stage, sem
):
    copies = [
        pltpu.make_async_copy(scores_hbm, scores, sem.at[0]),
        pltpu.make_async_copy(probes_hbm, probes, sem.at[1]),
        pltpu.make_async_copy(ranked_hbm, ranked, sem.at[2]),
    ]
    for copy in copies:
        copy.start()
    copies[1].wait()
    copies[0].wait()
    stage[...] = scores[...].astype(F32).reshape(L * ROWS, 128)
    for u in range(USERS):
        hot = jnp.where(iota((L, PROBES), 0) == probes[u : u + 1, :], 1.0, 0.0).astype(BF16)
        found = [stage[pl.ds(u * G + g, L, stride=ROWS), :].astype(BF16) for g in range(G)]
        list_scores[u] = dot_first(hot, jnp.concatenate(found, axis=1)).astype(BF16)
    copies[2].wait()


def shards(
    user_vectors,
    probe_lists,
    list_items,
    candidate_ids,
    history,
    history_lengths,
    query_weight,
    key_value_weight,
    out_weight,
):
    vmem = pl.BlockSpec(memory_space=pltpu.VMEM)
    hbm = pl.BlockSpec(memory_space=pl.ANY)
    scores_in, ranked = pl.pallas_call(
        kernel,
        out_shape=(
            jax.ShapeDtypeStruct((L, ROWS, 128), BF16),
            jax.ShapeDtypeStruct((OWN, D), BF16),
        ),
        in_specs=[hbm] * 8,
        out_specs=(hbm, vmem),
        scratch_shapes=[
            pltpu.VMEM((1, CANDS), jnp.int32),
            pltpu.SMEM((1,), jnp.int32),
            pltpu.VMEM((USERS, D), BF16),
            pltpu.VMEM((ITEMS, D), BF16),
            pltpu.VMEM((D, D), BF16),
            pltpu.VMEM((D, 2 * D), BF16),
            pltpu.VMEM((D, D), BF16),
            pltpu.VMEM((U, EVENTS, D), BF16),
            pltpu.VMEM((HIST, 2 * D), BF16),
            pltpu.VMEM((CANDS, 4 * L), BF16),
            pltpu.VMEM((L, 128), F32),
            pltpu.VMEM((L, 1, 128), F32),
            pltpu.VMEM((L, 1, 128), F32),
            pltpu.VMEM((1, 1, 256), F32),
            pltpu.VMEM((Z, 1, 256), F32),
            pltpu.VMEM((Z, 256), F32),
            pltpu.VMEM((4, Z, 256), BF16),
            pltpu.VMEM((U, L, 256), BF16),
            pltpu.VMEM((L * ROWS, 128), F32),
            pltpu.VMEM((L, ROWS, 128), BF16),
            pltpu.VMEM((L, ROWS, 128), BF16),
            pltpu.VMEM((L, ROWS, 128), BF16),
            pltpu.VMEM((X, OWN, D), BF16),
            pltpu.VMEM((X, OWN, D), BF16),
            pltpu.VMEM((2 * X, OWN, D), BF16),
            pltpu.VMEM((4 * L, D), BF16),
            pltpu.SemaphoreType.DMA((9,)),
            pltpu.SemaphoreType.DMA((10,)),
            pltpu.SemaphoreType.DMA((10,)),
            pltpu.SemaphoreType.REGULAR,
        ],
        compiler_params=pltpu.CompilerParams(
            collective_id=0, has_side_effects=True, vmem_limit_bytes=56 * 2**20
        ),
        cost_estimate=pl.CostEstimate(
            flops=2 * 10**9, bytes_accessed=4 * 10**6, transcendentals=600000
        ),
    )(
        candidate_ids,
        history_lengths,
        user_vectors,
        list_items.reshape(ITEMS, D),
        history.reshape(EVENTS, D),
        query_weight,
        key_value_weight,
        out_weight,
    )
    list_scores, ranked = pl.pallas_call(
        finish,
        out_shape=(
            jax.ShapeDtypeStruct((USERS, PROBES, ITEMS), BF16),
            jax.ShapeDtypeStruct((OWN, D), BF16),
        ),
        in_specs=[hbm] * 3,
        out_specs=(vmem, vmem),
        scratch_shapes=[
            pltpu.VMEM((USERS, PROBES), jnp.int32),
            pltpu.VMEM((L, ROWS, 128), BF16),
            pltpu.VMEM((L * ROWS, 128), F32),
            pltpu.SemaphoreType.DMA((3,)),
        ],
        compiler_params=pltpu.CompilerParams(vmem_limit_bytes=56 * 2**20),
        cost_estimate=pl.CostEstimate(flops=2 * 10**7, bytes_accessed=10**6, transcendentals=0),
    )(probe_lists, scores_in, ranked)
    return list_scores, ranked.reshape(1, OWN, D)


def solution(mesh):
    placed = (
        P("lists", None),
        P("lists", None),
        P("lists", "users", None),
        P("lists", None),
        P("lists", "users", None),
        P("lists"),
        P(),
        P(),
        P(),
    )
    return jax.shard_map(
        shards,
        mesh=mesh,
        in_specs=placed,
        out_specs=(P("lists", None, "users"), P("lists", "users", None)),
        check_vma=False,
    )
```

```python
import jax
import jax.numpy as jnp
from jax import lax
from jax.experimental import pallas as pl
from jax.experimental.pallas import tpu as pltpu
from jax.sharding import PartitionSpec as P

MESH = pl.DeviceIdType.MESH
F32 = jnp.float32
BF16 = jnp.bfloat16

L = 64
Z = 16
U = 8
X = 4
USERS = 4
PROBES = 32
ITEMS = 512
D = 512
SLOTS = 3
CANDS = 512
OWN = CANDS // U
EVENTS = 128
HIST = U * EVENTS
HEADS = 8
G = D // 128
ROWS = 16


def dot(a, b):
    return jnp.dot(a, b, preferred_element_type=F32)


def dot_first(a, b):
    return lax.dot_general(a, b, (((0,), (0,)), ((), ())), preferred_element_type=F32)


def dot_last(a, b):
    return lax.dot_general(a, b, (((1,), (1,)), ((), ())), preferred_element_type=F32)


def iota(shape, dim):
    return lax.broadcasted_iota(jnp.int32, shape, dim)


def kernel(
    ids_hbm,
    length_hbm,
    users_hbm,
    items_hbm,
    history_hbm,
    wq_hbm,
    wkv_hbm,
    wo_hbm,
    scores_in,
    ranked,
    ids,
    length,
    users,
    items,
    wq,
    wkv,
    wo,
    history,
    pairs,
    select,
    request,
    ask,
    asked,
    part,
    parts,
    user_part,
    user_plane,
    user_all,
    stage,
    rows_out,
    rows_in,
    scores_out,
    placed,
    swap,
    spread,
    gathered,
    local_sem,
    send_sem,
    recv_sem,
    heard,
):
    me = lax.axis_index("lists")
    col = lax.axis_index("users")
    chip, core = lax.div(col, 2), lax.rem(col, 2)
    plane, row = lax.div(me, 4), lax.rem(me, 4)

    def local(source, target, at):
        return pltpu.make_async_copy(source, target, local_sem.at[at])

    get_ids = local(ids_hbm, ids, 0)
    get_users = local(users_hbm, users, 1)
    get_history = local(history_hbm, history.at[col], 2)
    get_items = local(items_hbm, items, 3)
    get_rest = [
        local(wkv_hbm, wkv, 4),
        local(wq_hbm, wq, 5),
        local(wo_hbm, wo, 6),
        local(length_hbm, length, 7),
    ]
    get_ids.start()
    get_users.start()
    get_history.start()

    barrier = pltpu.get_barrier_semaphore()

    def over_z(d):
        return lax.rem(me + 4 * d, L)

    def over_y(d):
        return me - row + lax.rem(row + d, 4)

    for d in range(1, Z):
        pl.semaphore_signal(barrier, inc=1, device_id=(over_z(d), col), device_id_type=MESH)
    for d in range(1, 4):
        pl.semaphore_signal(barrier, inc=1, device_id=(over_y(d), col), device_id_type=MESH)

    @pl.loop(1, U)
    def _(d):
        pl.semaphore_signal(
            barrier, inc=1, device_id=(me, lax.rem(col + d, U)), device_id_type=MESH
        )

    get_items.start()
    for copy in get_rest:
        copy.start()

    get_ids.wait()
    wanted = ids[...]
    mine = lax.shift_right_logical(wanted, 9) == iota((L, CANDS), 0) * U + col
    mine = jnp.where(mine, 1.0, 0.0).astype(F32)
    place = jnp.bitwise_and(wanted, ITEMS - 1).astype(F32)
    earlier = jnp.where(iota((CANDS, CANDS), 0) < iota((CANDS, CANDS), 1), 1.0, 0.0)
    before = dot(mine.astype(BF16), earlier.astype(BF16))
    lane = iota((L, 128), 1)
    line = jnp.zeros((L, 128), F32)
    slots = []
    for k in range(SLOTS):
        slots.append(jnp.where(before == k, mine, 0.0))
        line = jnp.where(lane == k, jnp.sum(slots[k] * place, axis=1, keepdims=True), line)
    request[...] = line

    for p in range(L):
        ask[p] = request[p : p + 1, :]

    get_users.wait()
    vectors = users[...].astype(F32)
    half = jnp.where(core == 0, vectors[:, :256], vectors[:, 256:])
    part[0] = jnp.sum(jnp.where(iota((USERS, 256), 0) == chip, half, 0.0), axis=0, keepdims=True)
    get_history.wait()
    pl.semaphore_wait(barrier, Z - 1 + 4 - 1 + U - 1)
    for d in range(1, 4):
        pl.semaphore_signal(heard, inc=1, device_id=(over_y(d), col), device_id_type=MESH)
    pl.semaphore_wait(heard, 4 - 1)

    def to_rows(source, target, at, order):
        def send(p):
            pltpu.make_async_remote_copy(
                source(p),
                target.at[me],
                send_sem.at[at],
                recv_sem.at[at],
                device_id=(p, col),
                device_id_type=MESH,
            ).start()

        if order is None:

            @pl.loop(1, L)
            def _(d):
                send(jnp.bitwise_and(me + d, L - 1))

        else:
            for first, count, rotate in order:
                @pl.loop(0, 4 * count)
                def _(i):
                    if rotate:
                        i = lax.rem(i + me + 4 * rotate, 4 * count)
                    p = 4 * first + i
                    @pl.when(p != me)
                    def _():
                        send(p)

    def to_chips(source, target, at):
        @pl.loop(1, X)
        def _(d):
            there = lax.rem(chip + d, X)
            pltpu.make_async_remote_copy(
                source(there),
                target(d),
                send_sem.at[at],
                recv_sem.at[at],
                device_id=(me, 2 * there + core),
                device_id_type=MESH,
            ).start()

    def to_core(source, target, at):
        return pltpu.make_async_remote_copy(
            source,
            target,
            send_sem.at[at],
            recv_sem.at[at],
            device_id=(me, 2 * chip + 1 - core),
            device_id_type=MESH,
        )

    def wait_all(target, count, sem):
        some = target.at[pl.ds(0, count)]
        pltpu.make_async_copy(some, some, sem).wait()

    to_rows(lambda p: ask.at[p], asked, 0, [(8, 8, 1), (0, 8, 1)])
    to_chips(lambda there: history.at[col], lambda d: history.at[col], 1)
    for d in range(1, Z):
        pltpu.make_async_remote_copy(
            part.at[0],
            parts.at[plane],
            send_sem.at[2],
            recv_sem.at[2],
            device_id=(over_z(d), col),
            device_id_type=MESH,
        ).start()
    asked[me] = ask[me]
    parts[plane] = part[0]

    turned = jnp.concatenate(slots + [jnp.zeros((L, CANDS), F32)], axis=0).T.astype(BF16)
    for c in range(U):
        at = (c % 2) * X + c // 2
        select[at * OWN : (at + 1) * OWN, :] = turned[c * OWN : (c + 1) * OWN, :]
    gathered[SLOTS * L :, :] = jnp.zeros((L, D), BF16)
    stage[...] = jnp.zeros_like(stage)

    get_items.wait()
    wait_all(asked, L - 1, recv_sem.at[0])

    for p in range(L):
        request[p : p + 1, :] = asked[p]
    asks = request[...]
    for k in range(SLOTS):
        hot = jnp.where(asks[:, k : k + 1] == iota((L, ITEMS), 1).astype(F32), 1.0, 0.0)
        found = dot(hot.astype(BF16), items[...])
        for g in range(G):
            stage[pl.ds(k * G + g, L, stride=ROWS), :] = found[:, g * 128 : (g + 1) * 128]
    for first, last in ((0, 16), (16, L)):
        part_of = stage[first * ROWS : last * ROWS, :]
        rows_out[first:last] = part_of.reshape(last - first, ROWS, 128).astype(BF16)
        to_rows(lambda p: rows_out.at[p], rows_in, 3, [(first // 4, (last - first) // 4, 1)])
    rows_in[me] = rows_out[me]

    wait_all(parts, Z - 1, recv_sem.at[2])
    for z in range(Z):
        user_part[z : z + 1, :] = parts[z]
    user_plane[row] = user_part[...].astype(BF16)
    for d in range(1, 4):
        pltpu.make_async_remote_copy(
            user_plane.at[row],
            user_plane.at[row],
            send_sem.at[9],
            recv_sem.at[9],
            device_id=(over_y(d), col),
            device_id_type=MESH,
        ).start()

    wait_all(history, X - 1, recv_sem.at[1])

    @pl.loop(0, X)
    def _(x):
        to_core(history.at[2 * x + core], history.at[2 * x + core], 5).start()

    wait_all(user_plane, 4 - 1, recv_sem.at[9])
    user_all[col] = user_plane[...].reshape(L, 256)

    @pl.loop(1, U)
    def _(d):
        pltpu.make_async_remote_copy(
            user_all.at[col],
            user_all.at[col],
            send_sem.at[4],
            recv_sem.at[4],
            device_id=(me, lax.rem(col + d, U)),
            device_id_type=MESH,
        ).start()

    for copy in get_rest:
        copy.wait()
    wait_all(history, X, recv_sem.at[5])

    @pl.loop(0, U)
    def _(c):
        pairs[pl.ds(pl.multiple_of(c * EVENTS, EVENTS), EVENTS), :] = dot(
            history[c], wkv[...]
        ).astype(BF16)

    wait_all(user_all, U - 1, recv_sem.at[4])
    for u in range(USERS):
        found = dot_last(user_all[2 * u], items[:, 0:256]) + dot_last(
            user_all[2 * u + 1], items[:, 256:512]
        )
        found = found * D ** (-0.5)
        for y in range(4):
            for g in range(G):
                stage[pl.ds(y * ROWS + u * G + g, Z, stride=4 * ROWS), :] = found[
                    y * Z : (y + 1) * Z, g * 128 : (g + 1) * 128
                ]
    scores_out[...] = stage[...].reshape(L, ROWS, 128).astype(BF16)
    keep = local(scores_out.at[me], scores_in.at[me], 8)
    keep.start()
    to_rows(lambda p: scores_out.at[p], scores_in, 6, [(0, 16, 0)])

    wait_all(rows_in, L - 1, recv_sem.at[3])
    stage[...] = rows_in[...].astype(F32).reshape(L * ROWS, 128)
    for k in range(SLOTS):
        for g in range(G):
            gathered[k * L : (k + 1) * L, g * 128 : (g + 1) * 128] = stage[
                pl.ds(k * G + g, L, stride=ROWS), :
            ].astype(BF16)

    def spots(c):
        block = select[pl.ds(pl.multiple_of(c * X * OWN, X * OWN), X * OWN), :]
        return dot(block, gathered[...])

    placed[...] = spots(1 - core).astype(BF16).reshape(X, OWN, D)
    pair = to_core(placed, swap, 7)
    pair.start()
    kept = spots(core).reshape(X, OWN, D)
    pair.wait_recv()
    spread[0:X] = (kept + swap[...].astype(F32)).astype(BF16)
    to_chips(lambda there: spread.at[there], lambda d: spread.at[X + d], 8)
    wait_all(spread, X - 1, recv_sem.at[8])
    cand = spread[chip].astype(F32)
    for d in range(1, X):
        cand = cand + spread[X + d].astype(F32)

    queries = (dot(cand.astype(BF16), wq[...]) * (D // HEADS) ** (-0.5)).astype(BF16)
    low = iota((OWN, 128), 1) < 64
    valid = iota((1, HIST), 1) < length[0]
    nothing = jnp.zeros((OWN, 128), BF16)
    attended = []
    for j in range(HEADS // 2):
        two = queries[:, j * 128 : (j + 1) * 128]
        two = jnp.concatenate([jnp.where(low, two, nothing), jnp.where(low, nothing, two)], axis=0)
        scores = dot_last(two, pairs[:, j * 128 : (j + 1) * 128])
        scores = jnp.where(valid, scores, F32(-1e30))
        top = jnp.max(scores, axis=1, keepdims=True)
        powers = jnp.where(valid, jnp.exp(scores - top), 0.0)
        total = jnp.sum(powers, axis=1, keepdims=True)
        mixed = dot(powers.astype(BF16), pairs[:, D + j * 128 : D + (j + 1) * 128]) / total
        attended.append(jnp.where(low, mixed[:OWN], mixed[OWN:]).astype(BF16))
    ranked[...] = dot(jnp.concatenate(attended, axis=1), wo[...]).astype(BF16)

    wait_all(asked, L - 1, send_sem.at[0])
    wait_all(history, X - 1, send_sem.at[1])
    wait_all(parts, Z - 1, send_sem.at[2])
    wait_all(user_plane, 4 - 1, send_sem.at[9])
    wait_all(rows_in, L - 1, send_sem.at[3])
    wait_all(user_all, U - 1, send_sem.at[4])
    wait_all(history, X, send_sem.at[5])
    pair.wait_send()
    wait_all(spread, X - 1, send_sem.at[8])
    keep.wait()
    wait_all(scores_in, L - 1, send_sem.at[6])
    wait_all(scores_in, L - 1, recv_sem.at[6])


def finish(
    probes_hbm, scores_hbm, ranked_hbm, list_scores, ranked, probes, scores, stage, sem
):
    copies = [
        pltpu.make_async_copy(scores_hbm, scores, sem.at[0]),
        pltpu.make_async_copy(probes_hbm, probes, sem.at[1]),
        pltpu.make_async_copy(ranked_hbm, ranked, sem.at[2]),
    ]
    for copy in copies:
        copy.start()
    copies[1].wait()
    copies[0].wait()
    stage[...] = scores[...].astype(F32).reshape(L * ROWS, 128)
    for u in range(USERS):
        hot = jnp.where(iota((L, PROBES), 0) == probes[u : u + 1, :], 1.0, 0.0).astype(BF16)
        found = [stage[pl.ds(u * G + g, L, stride=ROWS), :].astype(BF16) for g in range(G)]
        list_scores[u] = dot_first(hot, jnp.concatenate(found, axis=1)).astype(BF16)
    copies[2].wait()


def shards(
    user_vectors,
    probe_lists,
    list_items,
    candidate_ids,
    history,
    history_lengths,
    query_weight,
    key_value_weight,
    out_weight,
):
    vmem = pl.BlockSpec(memory_space=pltpu.VMEM)
    hbm = pl.BlockSpec(memory_space=pl.ANY)
    scores_in, ranked = pl.pallas_call(
        kernel,
        out_shape=(
            jax.ShapeDtypeStruct((L, ROWS, 128), BF16),
            jax.ShapeDtypeStruct((OWN, D), BF16),
        ),
        in_specs=[hbm] * 8,
        out_specs=(hbm, vmem),
        scratch_shapes=[
            pltpu.VMEM((1, CANDS), jnp.int32),
            pltpu.SMEM((1,), jnp.int32),
            pltpu.VMEM((USERS, D), BF16),
            pltpu.VMEM((ITEMS, D), BF16),
            pltpu.VMEM((D, D), BF16),
            pltpu.VMEM((D, 2 * D), BF16),
            pltpu.VMEM((D, D), BF16),
            pltpu.VMEM((U, EVENTS, D), BF16),
            pltpu.VMEM((HIST, 2 * D), BF16),
            pltpu.VMEM((CANDS, 4 * L), BF16),
            pltpu.VMEM((L, 128), F32),
            pltpu.VMEM((L, 1, 128), F32),
            pltpu.VMEM((L, 1, 128), F32),
            pltpu.VMEM((1, 1, 256), F32),
            pltpu.VMEM((Z, 1, 256), F32),
            pltpu.VMEM((Z, 256), F32),
            pltpu.VMEM((4, Z, 256), BF16),
            pltpu.VMEM((U, L, 256), BF16),
            pltpu.VMEM((L * ROWS, 128), F32),
            pltpu.VMEM((L, ROWS, 128), BF16),
            pltpu.VMEM((L, ROWS, 128), BF16),
            pltpu.VMEM((L, ROWS, 128), BF16),
            pltpu.VMEM((X, OWN, D), BF16),
            pltpu.VMEM((X, OWN, D), BF16),
            pltpu.VMEM((2 * X, OWN, D), BF16),
            pltpu.VMEM((4 * L, D), BF16),
            pltpu.SemaphoreType.DMA((9,)),
            pltpu.SemaphoreType.DMA((10,)),
            pltpu.SemaphoreType.DMA((10,)),
            pltpu.SemaphoreType.REGULAR,
        ],
        compiler_params=pltpu.CompilerParams(
            collective_id=0, has_side_effects=True, vmem_limit_bytes=56 * 2**20
        ),
        cost_estimate=pl.CostEstimate(
            flops=2 * 10**9, bytes_accessed=4 * 10**6, transcendentals=600000
        ),
    )(
        candidate_ids,
        history_lengths,
        user_vectors,
        list_items.reshape(ITEMS, D),
        history.reshape(EVENTS, D),
        query_weight,
        key_value_weight,
        out_weight,
    )
    list_scores, ranked = pl.pallas_call(
        finish,
        out_shape=(
            jax.ShapeDtypeStruct((USERS, PROBES, ITEMS), BF16),
            jax.ShapeDtypeStruct((OWN, D), BF16),
        ),
        in_specs=[hbm] * 3,
        out_specs=(vmem, vmem),
        scratch_shapes=[
            pltpu.VMEM((USERS, PROBES), jnp.int32),
            pltpu.VMEM((L, ROWS, 128), BF16),
            pltpu.VMEM((L * ROWS, 128), F32),
            pltpu.SemaphoreType.DMA((3,)),
        ],
        compiler_params=pltpu.CompilerParams(vmem_limit_bytes=56 * 2**20),
        cost_estimate=pl.CostEstimate(flops=2 * 10**7, bytes_accessed=10**6, transcendentals=0),
    )(probe_lists, scores_in, ranked)
    return list_scores, ranked.reshape(1, OWN, D)


def solution(mesh):
    placed = (
        P("lists", None),
        P("lists", None),
        P("lists", "users", None),
        P("lists", None),
        P("lists", "users", None),
        P("lists"),
        P(),
        P(),
        P(),
    )
    return jax.shard_map(
        shards,
        mesh=mesh,
        in_specs=placed,
        out_specs=(P("lists", None, "users"), P("lists", "users", None)),
        check_vma=False,
    )
```

```python
import jax
import jax.numpy as jnp
from jax import lax
from jax.experimental import pallas as pl
from jax.experimental.pallas import tpu as pltpu
from jax.sharding import PartitionSpec as P

MESH = pl.DeviceIdType.MESH
F32 = jnp.float32
BF16 = jnp.bfloat16

L = 64
Z = 16
U = 8
X = 4
USERS = 4
PROBES = 32
ITEMS = 512
D = 512
SLOTS = 3
CANDS = 512
OWN = CANDS // U
EVENTS = 128
HIST = U * EVENTS
HEADS = 8
G = D // 128
ROWS = 16


def dot(a, b):
    return jnp.dot(a, b, preferred_element_type=F32)


def dot_first(a, b):
    return lax.dot_general(a, b, (((0,), (0,)), ((), ())), preferred_element_type=F32)


def dot_last(a, b):
    return lax.dot_general(a, b, (((1,), (1,)), ((), ())), preferred_element_type=F32)


def iota(shape, dim):
    return lax.broadcasted_iota(jnp.int32, shape, dim)


def kernel(
    ids_hbm,
    length_hbm,
    users_hbm,
    items_hbm,
    history_hbm,
    wq_hbm,
    wkv_hbm,
    wo_hbm,
    scores_in,
    ranked,
    ids,
    length,
    users,
    items,
    wq,
    wkv,
    wo,
    history,
    pairs,
    select,
    request,
    ask,
    asked,
    part,
    parts,
    user_part,
    user_plane,
    user_all,
    stage,
    rows_out,
    rows_in,
    scores_out,
    placed,
    swap,
    spread,
    gathered,
    local_sem,
    send_sem,
    recv_sem,
    heard,
):
    me = lax.axis_index("lists")
    col = lax.axis_index("users")
    chip, core = lax.div(col, 2), lax.rem(col, 2)
    plane, row = lax.div(me, 4), lax.rem(me, 4)

    def local(source, target, at):
        return pltpu.make_async_copy(source, target, local_sem.at[at])

    get_ids = local(ids_hbm, ids, 0)
    get_users = local(users_hbm, users, 1)
    get_history = local(history_hbm, history.at[col], 2)
    get_items = local(items_hbm, items, 3)
    get_rest = [
        local(wkv_hbm, wkv, 4),
        local(wq_hbm, wq, 5),
        local(wo_hbm, wo, 6),
        local(length_hbm, length, 7),
    ]
    get_ids.start()
    get_users.start()
    get_history.start()

    barrier = pltpu.get_barrier_semaphore()

    def over_z(d):
        return lax.rem(me + 4 * d, L)

    def over_y(d):
        return me - row + lax.rem(row + d, 4)

    for d in range(1, Z):
        pl.semaphore_signal(barrier, inc=1, device_id=(over_z(d), col), device_id_type=MESH)
    for d in range(1, 4):
        pl.semaphore_signal(barrier, inc=1, device_id=(over_y(d), col), device_id_type=MESH)

    @pl.loop(1, U)
    def _(d):
        pl.semaphore_signal(
            barrier, inc=1, device_id=(me, lax.rem(col + d, U)), device_id_type=MESH
        )

    get_items.start()
    for copy in get_rest:
        copy.start()

    get_ids.wait()
    wanted = ids[...]
    mine = lax.shift_right_logical(wanted, 9) == iota((L, CANDS), 0) * U + col
    mine = jnp.where(mine, 1.0, 0.0).astype(F32)
    place = jnp.bitwise_and(wanted, ITEMS - 1).astype(F32)
    earlier = jnp.where(iota((CANDS, CANDS), 0) < iota((CANDS, CANDS), 1), 1.0, 0.0)
    before = dot(mine.astype(BF16), earlier.astype(BF16))
    lane = iota((L, 128), 1)
    line = jnp.zeros((L, 128), F32)
    slots = []
    for k in range(SLOTS):
        slots.append(jnp.where(before == k, mine, 0.0))
        line = jnp.where(lane == k, jnp.sum(slots[k] * place, axis=1, keepdims=True), line)
    request[...] = line

    for p in range(L):
        ask[p] = request[p : p + 1, :]

    get_users.wait()
    vectors = users[...].astype(F32)
    half = jnp.where(core == 0, vectors[:, :256], vectors[:, 256:])
    part[0] = jnp.sum(jnp.where(iota((USERS, 256), 0) == chip, half, 0.0), axis=0, keepdims=True)
    get_history.wait()
    pl.semaphore_wait(barrier, Z - 1 + 4 - 1 + U - 1)
    for d in range(1, 4):
        pl.semaphore_signal(heard, inc=1, device_id=(over_y(d), col), device_id_type=MESH)
    pl.semaphore_wait(heard, 4 - 1)

    def to_rows(source, target, at, order):
        def send(p):
            pltpu.make_async_remote_copy(
                source(p),
                target.at[me],
                send_sem.at[at],
                recv_sem.at[at],
                device_id=(p, col),
                device_id_type=MESH,
            ).start()

        if order is None:

            @pl.loop(1, L)
            def _(d):
                send(jnp.bitwise_and(me + d, L - 1))

        else:
            for first, count, rotate in order:
                @pl.loop(0, 4 * count)
                def _(i):
                    if rotate:
                        i = lax.rem(i + me + 4 * rotate, 4 * count)
                    p = 4 * first + i
                    @pl.when(p != me)
                    def _():
                        send(p)

    def to_chips(source, target, at):
        @pl.loop(1, X)
        def _(d):
            there = lax.rem(chip + d, X)
            pltpu.make_async_remote_copy(
                source(there),
                target(d),
                send_sem.at[at],
                recv_sem.at[at],
                device_id=(me, 2 * there + core),
                device_id_type=MESH,
            ).start()

    def to_core(source, target, at):
        return pltpu.make_async_remote_copy(
            source,
            target,
            send_sem.at[at],
            recv_sem.at[at],
            device_id=(me, 2 * chip + 1 - core),
            device_id_type=MESH,
        )

    def wait_all(target, count, sem):
        some = target.at[pl.ds(0, count)]
        pltpu.make_async_copy(some, some, sem).wait()

    to_rows(lambda p: ask.at[p], asked, 0, [(8, 8, 1), (0, 8, 1)])
    to_chips(lambda there: history.at[col], lambda d: history.at[col], 1)
    for d in range(1, Z):
        pltpu.make_async_remote_copy(
            part.at[0],
            parts.at[plane],
            send_sem.at[2],
            recv_sem.at[2],
            device_id=(over_z(d), col),
            device_id_type=MESH,
        ).start()
    asked[me] = ask[me]
    parts[plane] = part[0]

    turned = jnp.concatenate(slots + [jnp.zeros((L, CANDS), F32)], axis=0).T.astype(BF16)
    for c in range(U):
        at = (c % 2) * X + c // 2
        select[at * OWN : (at + 1) * OWN, :] = turned[c * OWN : (c + 1) * OWN, :]
    gathered[SLOTS * L :, :] = jnp.zeros((L, D), BF16)
    stage[...] = jnp.zeros_like(stage)

    get_items.wait()
    wait_all(asked, L - 1, recv_sem.at[0])

    for p in range(L):
        request[p : p + 1, :] = asked[p]
    asks = request[...]
    for k in range(SLOTS):
        hot = jnp.where(asks[:, k : k + 1] == iota((L, ITEMS), 1).astype(F32), 1.0, 0.0)
        found = dot(hot.astype(BF16), items[...])
        for g in range(G):
            stage[pl.ds(k * G + g, L, stride=ROWS), :] = found[:, g * 128 : (g + 1) * 128]
    for first, last in ((0, 8), (8, 24), (24, L)):
        part_of = stage[first * ROWS : last * ROWS, :]
        rows_out[first:last] = part_of.reshape(last - first, ROWS, 128).astype(BF16)
        to_rows(lambda p: rows_out.at[p], rows_in, 3, [(first // 4, (last - first) // 4, 1)])
    rows_in[me] = rows_out[me]

    wait_all(parts, Z - 1, recv_sem.at[2])
    for z in range(Z):
        user_part[z : z + 1, :] = parts[z]
    user_plane[row] = user_part[...].astype(BF16)
    for d in range(1, 4):
        pltpu.make_async_remote_copy(
            user_plane.at[row],
            user_plane.at[row],
            send_sem.at[9],
            recv_sem.at[9],
            device_id=(over_y(d), col),
            device_id_type=MESH,
        ).start()

    wait_all(history, X - 1, recv_sem.at[1])

    @pl.loop(0, X)
    def _(x):
        to_core(history.at[2 * x + core], history.at[2 * x + core], 5).start()

    wait_all(user_plane, 4 - 1, recv_sem.at[9])
    user_all[col] = user_plane[...].reshape(L, 256)

    @pl.loop(1, U)
    def _(d):
        pltpu.make_async_remote_copy(
            user_all.at[col],
            user_all.at[col],
            send_sem.at[4],
            recv_sem.at[4],
            device_id=(me, lax.rem(col + d, U)),
            device_id_type=MESH,
        ).start()

    for copy in get_rest:
        copy.wait()
    wait_all(history, X, recv_sem.at[5])

    @pl.loop(0, U)
    def _(c):
        pairs[pl.ds(pl.multiple_of(c * EVENTS, EVENTS), EVENTS), :] = dot(
            history[c], wkv[...]
        ).astype(BF16)

    wait_all(user_all, U - 1, recv_sem.at[4])
    for u in range(USERS):
        found = dot_last(user_all[2 * u], items[:, 0:256]) + dot_last(
            user_all[2 * u + 1], items[:, 256:512]
        )
        found = found * D ** (-0.5)
        for y in range(4):
            for g in range(G):
                stage[pl.ds(y * ROWS + u * G + g, Z, stride=4 * ROWS), :] = found[
                    y * Z : (y + 1) * Z, g * 128 : (g + 1) * 128
                ]
    scores_out[...] = stage[...].reshape(L, ROWS, 128).astype(BF16)
    keep = local(scores_out.at[me], scores_in.at[me], 8)
    keep.start()
    to_rows(lambda p: scores_out.at[p], scores_in, 6, [(0, 16, 0)])

    wait_all(rows_in, L - 1, recv_sem.at[3])
    stage[...] = rows_in[...].astype(F32).reshape(L * ROWS, 128)
    for k in range(SLOTS):
        for g in range(G):
            gathered[k * L : (k + 1) * L, g * 128 : (g + 1) * 128] = stage[
                pl.ds(k * G + g, L, stride=ROWS), :
            ].astype(BF16)

    def spots(c):
        block = select[pl.ds(pl.multiple_of(c * X * OWN, X * OWN), X * OWN), :]
        return dot(block, gathered[...])

    placed[...] = spots(1 - core).astype(BF16).reshape(X, OWN, D)
    pair = to_core(placed, swap, 7)
    pair.start()
    kept = spots(core).reshape(X, OWN, D)
    pair.wait_recv()
    spread[0:X] = (kept + swap[...].astype(F32)).astype(BF16)
    to_chips(lambda there: spread.at[there], lambda d: spread.at[X + d], 8)
    wait_all(spread, X - 1, recv_sem.at[8])
    cand = spread[chip].astype(F32)
    for d in range(1, X):
        cand = cand + spread[X + d].astype(F32)

    queries = (dot(cand.astype(BF16), wq[...]) * (D // HEADS) ** (-0.5)).astype(BF16)
    low = iota((OWN, 128), 1) < 64
    valid = iota((1, HIST), 1) < length[0]
    nothing = jnp.zeros((OWN, 128), BF16)
    attended = []
    for j in range(HEADS // 2):
        two = queries[:, j * 128 : (j + 1) * 128]
        two = jnp.concatenate([jnp.where(low, two, nothing), jnp.where(low, nothing, two)], axis=0)
        scores = dot_last(two, pairs[:, j * 128 : (j + 1) * 128])
        scores = jnp.where(valid, scores, F32(-1e30))
        top = jnp.max(scores, axis=1, keepdims=True)
        powers = jnp.where(valid, jnp.exp(scores - top), 0.0)
        total = jnp.sum(powers, axis=1, keepdims=True)
        mixed = dot(powers.astype(BF16), pairs[:, D + j * 128 : D + (j + 1) * 128]) / total
        attended.append(jnp.where(low, mixed[:OWN], mixed[OWN:]).astype(BF16))
    ranked[...] = dot(jnp.concatenate(attended, axis=1), wo[...]).astype(BF16)

    wait_all(asked, L - 1, send_sem.at[0])
    wait_all(history, X - 1, send_sem.at[1])
    wait_all(parts, Z - 1, send_sem.at[2])
    wait_all(user_plane, 4 - 1, send_sem.at[9])
    wait_all(rows_in, L - 1, send_sem.at[3])
    wait_all(user_all, U - 1, send_sem.at[4])
    wait_all(history, X, send_sem.at[5])
    pair.wait_send()
    wait_all(spread, X - 1, send_sem.at[8])
    keep.wait()
    wait_all(scores_in, L - 1, send_sem.at[6])
    wait_all(scores_in, L - 1, recv_sem.at[6])


def finish(
    probes_hbm, scores_hbm, ranked_hbm, list_scores, ranked, probes, scores, stage, sem
):
    copies = [
        pltpu.make_async_copy(scores_hbm, scores, sem.at[0]),
        pltpu.make_async_copy(probes_hbm, probes, sem.at[1]),
        pltpu.make_async_copy(ranked_hbm, ranked, sem.at[2]),
    ]
    for copy in copies:
        copy.start()
    copies[1].wait()
    copies[0].wait()
    stage[...] = scores[...].astype(F32).reshape(L * ROWS, 128)
    for u in range(USERS):
        hot = jnp.where(iota((L, PROBES), 0) == probes[u : u + 1, :], 1.0, 0.0).astype(BF16)
        found = [stage[pl.ds(u * G + g, L, stride=ROWS), :].astype(BF16) for g in range(G)]
        list_scores[u] = dot_first(hot, jnp.concatenate(found, axis=1)).astype(BF16)
    copies[2].wait()


def shards(
    user_vectors,
    probe_lists,
    list_items,
    candidate_ids,
    history,
    history_lengths,
    query_weight,
    key_value_weight,
    out_weight,
):
    vmem = pl.BlockSpec(memory_space=pltpu.VMEM)
    hbm = pl.BlockSpec(memory_space=pl.ANY)
    scores_in, ranked = pl.pallas_call(
        kernel,
        out_shape=(
            jax.ShapeDtypeStruct((L, ROWS, 128), BF16),
            jax.ShapeDtypeStruct((OWN, D), BF16),
        ),
        in_specs=[hbm] * 8,
        out_specs=(hbm, vmem),
        scratch_shapes=[
            pltpu.VMEM((1, CANDS), jnp.int32),
            pltpu.SMEM((1,), jnp.int32),
            pltpu.VMEM((USERS, D), BF16),
            pltpu.VMEM((ITEMS, D), BF16),
            pltpu.VMEM((D, D), BF16),
            pltpu.VMEM((D, 2 * D), BF16),
            pltpu.VMEM((D, D), BF16),
            pltpu.VMEM((U, EVENTS, D), BF16),
            pltpu.VMEM((HIST, 2 * D), BF16),
            pltpu.VMEM((CANDS, 4 * L), BF16),
            pltpu.VMEM((L, 128), F32),
            pltpu.VMEM((L, 1, 128), F32),
            pltpu.VMEM((L, 1, 128), F32),
            pltpu.VMEM((1, 1, 256), F32),
            pltpu.VMEM((Z, 1, 256), F32),
            pltpu.VMEM((Z, 256), F32),
            pltpu.VMEM((4, Z, 256), BF16),
            pltpu.VMEM((U, L, 256), BF16),
            pltpu.VMEM((L * ROWS, 128), F32),
            pltpu.VMEM((L, ROWS, 128), BF16),
            pltpu.VMEM((L, ROWS, 128), BF16),
            pltpu.VMEM((L, ROWS, 128), BF16),
            pltpu.VMEM((X, OWN, D), BF16),
            pltpu.VMEM((X, OWN, D), BF16),
            pltpu.VMEM((2 * X, OWN, D), BF16),
            pltpu.VMEM((4 * L, D), BF16),
            pltpu.SemaphoreType.DMA((9,)),
            pltpu.SemaphoreType.DMA((10,)),
            pltpu.SemaphoreType.DMA((10,)),
            pltpu.SemaphoreType.REGULAR,
        ],
        compiler_params=pltpu.CompilerParams(
            collective_id=0, has_side_effects=True, vmem_limit_bytes=56 * 2**20
        ),
        cost_estimate=pl.CostEstimate(
            flops=2 * 10**9, bytes_accessed=4 * 10**6, transcendentals=600000
        ),
    )(
        candidate_ids,
        history_lengths,
        user_vectors,
        list_items.reshape(ITEMS, D),
        history.reshape(EVENTS, D),
        query_weight,
        key_value_weight,
        out_weight,
    )
    list_scores, ranked = pl.pallas_call(
        finish,
        out_shape=(
            jax.ShapeDtypeStruct((USERS, PROBES, ITEMS), BF16),
            jax.ShapeDtypeStruct((OWN, D), BF16),
        ),
        in_specs=[hbm] * 3,
        out_specs=(vmem, vmem),
        scratch_shapes=[
            pltpu.VMEM((USERS, PROBES), jnp.int32),
            pltpu.VMEM((L, ROWS, 128), BF16),
            pltpu.VMEM((L * ROWS, 128), F32),
            pltpu.SemaphoreType.DMA((3,)),
        ],
        compiler_params=pltpu.CompilerParams(vmem_limit_bytes=56 * 2**20),
        cost_estimate=pl.CostEstimate(flops=2 * 10**7, bytes_accessed=10**6, transcendentals=0),
    )(probe_lists, scores_in, ranked)
    return list_scores, ranked.reshape(1, OWN, D)


def solution(mesh):
    placed = (
        P("lists", None),
        P("lists", None),
        P("lists", "users", None),
        P("lists", None),
        P("lists", "users", None),
        P("lists"),
        P(),
        P(),
        P(),
    )
    return jax.shard_map(
        shards,
        mesh=mesh,
        in_specs=placed,
        out_specs=(P("lists", None, "users"), P("lists", "users", None)),
        check_vma=False,
    )
```
